32 devices in a mesh: row: 4 (over y, x), col: 8 (over z, core).
Axes of the slice: x: 2, y: 2, z: 4, core: 2. Of those that a mesh axis runs over, the one named last changes fastest.
Arguments:
- ancestor: float32 [20480, 20480], P('row', 'col'), as said below
- factor_rows: float32 [2, 256, 20480], P(None, 'row', 'col'), may hold values from -6 to 6
- block_lists: int32 [2, 8], replicated, may hold values from 0 to 15, as said below
Outputs:
- inverse_panel: float32 [2, 20480, 256], P(None, ('row', 'col'))
- inverse_rows: float32 [2, 256, 20480], P(None, 'col', 'row')
The draws below stay inside these ranges and needn't reach their ends.
Inputs may be any that keep to these rules, and one draw needn't show every extreme that they name: `block_lists`: each row lists 8 distinct blocks in increasing order; the first block 0 and the last block 15 are in every row. ancestor is symmetric: ancestor[i, j] = ancestor[j, i].
All inputs are finite; a program needn't handle non-finite values.
Results may differ from the reference program's by a relative error of at most 0.000071.
Values sent between devices are 32-bit elements; how exact they have to be, the bound alone decides.
No kernel may reach another device: no remote copies, remote signals or barrier semaphores. Data moves between devices by JAX's collectives and lax.ppermute only.
A program may use at most 128 MiB of HBM per device.

```python
import math
import jax
import jax.numpy as jnp
from jax import lax

W = 256
BS = 1280
NB = 16
NLIST = 8
SIB = 2
NA = 20480


def draw_block_lists(key, part):
    chosen = []
    for member in range(SIB):
        shuffled = jax.random.permutation(jax.random.fold_in(key, member + 17), NB - 2)[:NLIST - 2]
        middle = (shuffled.astype(jnp.int32) + 1).astype(jnp.int32)
        picked = jnp.concatenate([jnp.zeros((1,), jnp.int32), middle, jnp.full((1,), NB - 1, jnp.int32)])
        chosen.append(jnp.sort(picked))
    return jnp.stack(chosen).astype(jnp.int32)


def draw_ancestor(key, part):
    base = jax.random.normal(jax.random.fold_in(key, 3), (NA, NA), jnp.float32)
    symmetric = jnp.clip((base + base.T) * math.sqrt(0.5), -6.0, 6.0)
    return symmetric * NA ** (-0.5)


def block_scale(stream_key, shape, pieces, low, top_value):
    factor_of = 1.0
    for axis_at, shards_of in pieces:
        heights = jax.random.uniform(jax.random.fold_in(jax.random.fold_in(stream_key, 6), axis_at), (shards_of,), jnp.float32, low / len(pieces), top_value / len(pieces))
        factor_of = factor_of * jnp.repeat(jnp.exp(heights), shape[axis_at] // shards_of).reshape((-1,) + (1,) * (len(shape) - 1 - axis_at))
    return factor_of


def gaussian(key, extent, width, bound, split=(), kind=jnp.bfloat16):
    result = jax.random.normal(key, extent, jnp.float32) * width
    if len(split) > 0:
        result = block_scale(key, extent, split, -0.22, 0.18) * result
    return jnp.clip(result, min=-bound, max=bound).astype(kind)


def setup_inputs(seed: int = 0) -> dict:
    seeds = jax.random.split(jax.random.key(seed), 4)
    ancestor = draw_ancestor(jax.random.fold_in(seeds[3], 71), 0)
    factor_rows = gaussian(seeds[1], (SIB, W, NA), 1.0, 6.0, ((1, 4), (2, 8)), jnp.float32)
    block_lists = draw_block_lists(jax.random.fold_in(seeds[3], 71), 0)
    return {"ancestor": ancestor, "factor_rows": factor_rows, "block_lists": block_lists}


def listed_mask(block_lists, blocks):
    return jnp.any(block_lists[:, :, None] == blocks[None, None, :], axis=1).astype(jnp.float32)


def reference(ancestor, factor_rows, block_lists):
    blocks = (jnp.arange(NB * BS, dtype=jnp.int32) // BS).astype(jnp.int32)
    listed = listed_mask(block_lists, blocks)
    masked = factor_rows * listed[:, None, :]
    product = jnp.einsum("ij,swj->siw", ancestor, masked, precision=lax.Precision.HIGHEST)
    inverse_panel = -product * listed[:, :, None]
    inverse_rows = jnp.transpose(inverse_panel, (0, 2, 1))
    return inverse_panel, inverse_rows
```

```python
import functools

import jax
import jax.numpy as jnp
from jax import lax
from jax.experimental import pallas as pl
from jax.experimental.pallas import tpu as pltpu
from jax.sharding import PartitionSpec as P

BS = 1280
F32 = jnp.float32
BF16 = jnp.bfloat16
I32 = jnp.int32
VMEM_LIMIT = 20 * 1024 * 1024
PARAMS = pltpu.CompilerParams(vmem_limit_bytes=VMEM_LIMIT)
LAGS = (0, 1, 3, 4)
PRODUCT_FLOPS = 0
OTHER_FLOPS = 0
RELAY_AFTER = 1
PLACE_EARLY = 99
PLACE_WAITS = False
SWAP_PARTS = 1
ANY = pl.BlockSpec(memory_space=pl.ANY)


def tile_of(extent, wanted, step):
    best = extent
    for size in range(step, wanted + 1, step):
        if extent % size == 0:
            best = size
    return best


def cost(bytes_accessed):
    return pl.CostEstimate(flops=OTHER_FLOPS, bytes_accessed=bytes_accessed, transcendentals=0)


def copy_kernel(source, target):
    target[...] = source[0]


def share_of(factor_rows, member):
    share, cols = factor_rows.shape[1:]
    return pl.pallas_call(
        copy_kernel,
        grid=(1,),
        in_specs=[pl.BlockSpec((1, share, cols), lambda i: (member, 0, 0))],
        out_specs=pl.BlockSpec((share, cols), lambda i: (0, 0)),
        out_shape=jax.ShapeDtypeStruct((share, cols), F32),
        compiler_params=PARAMS,
        cost_estimate=cost(1024),
        name="own_share",
    )(factor_rows)


def prep_kernel(places, share, following, base, units, bits, meta_ref, *refs):
    pieces = refs[: len(places)]
    rest = refs[len(places) :]
    if following:
        next_in, high_ref, low_ref, next_out, whole = rest
        next_out[...] = next_in[0]
    else:
        high_ref, low_ref, whole = rest
    me = meta_ref[base + 2]
    row = meta_ref[base + 3]
    step = pl.program_id(0)
    rows = whole.shape[0] >> bits
    for (mask, offset), piece in zip(places, pieces):
        first = (row ^ mask) * share + offset
        for at in range(0, piece.shape[0], rows):
            flip = ((first + at) // rows) ^ me
            turned_flip = sum(((flip >> bit) & 1) << (bits - 1 - bit) for bit in range(bits))
            whole[pl.ds(pl.multiple_of(turned_flip * rows, rows), rows), :] = piece[at : at + rows, :]
    scale = jnp.where(meta_ref[base + 4 + step] > 0, -1.0, 0.0).astype(F32)
    turned = whole[...].T * scale
    high = turned.astype(BF16)
    high_ref[...] = high
    low_ref[...] = (turned - high.astype(F32)).astype(BF16)


def prepare(base, meta, factor_rows, own, received, width, unit, bits, following):
    share, cols = own.shape
    units = cols // unit
    places = [(0, 0)] + [(mask, offset) for mask, offset, _ in received]
    arrays = [own] + [piece for _, _, piece in received]
    in_specs = [pl.BlockSpec((piece.shape[0], unit), lambda i, m: (0, i)) for piece in arrays]
    out_specs = [pl.BlockSpec((unit, width), lambda i, m: (i, 0))] * 2
    out_shape = [jax.ShapeDtypeStruct((cols, width), BF16)] * 2
    if following is not None:
        arrays.append(factor_rows)
        in_specs.append(pl.BlockSpec((1, share, unit), lambda i, m: (following, 0, i)))
        out_specs.append(pl.BlockSpec((share, unit), lambda i, m: (0, i)))
        out_shape.append(jax.ShapeDtypeStruct((share, cols), F32))
    outs = pl.pallas_call(
        functools.partial(prep_kernel, places, share, following is not None, base, units, bits),
        grid_spec=pltpu.PrefetchScalarGridSpec(
            num_scalar_prefetch=1,
            grid=(units,),
            in_specs=in_specs,
            out_specs=out_specs,
            scratch_shapes=[pltpu.VMEM((width, unit), F32)],
        ),
        out_shape=out_shape,
        compiler_params=PARAMS,
        cost_estimate=cost(1024),
        name="prepare_factor",
    )(meta, *arrays)
    return outs if following is not None else (*outs, None)


def slot_kernel(base, tile, deps, meta_ref, a_ref, high_ref, low_ref, *refs):
    mine_ref, theirs_ref, buffer, total, arrived = refs[deps:]
    half, rows, block = mine_ref.shape
    tiles = block // tile
    depth = buffer.shape[0]
    first = meta_ref[base] * block

    def copy(t):
        source = a_ref.at[pl.ds(pl.multiple_of(first + t * tile, tile), tile), :]
        slot = lax.rem(t, depth)
        return pltpu.make_async_copy(source, buffer.at[slot], arrived.at[slot])

    def turn(t):
        turned = total[lax.rem(t, 2)].T
        columns = pl.ds(pl.multiple_of(t * tile, tile), tile)
        mine_ref[:, :, columns] = turned[: half * rows].reshape(half, rows, tile)
        theirs_ref[:, :, columns] = turned[half * rows :].reshape(half, rows, tile)

    def product(t):
        a = buffer[lax.rem(t, depth)]
        a_high = a.astype(BF16)
        a_low = (a - a_high.astype(F32)).astype(BF16)
        dot = functools.partial(jnp.dot, preferred_element_type=F32)
        total[lax.rem(t, 2)] = (
            dot(a_high, high_ref[...]) + dot(a_high, low_ref[...]) + dot(a_low, high_ref[...])
        )

    valid = meta_ref[base + 1] > 0

    @pl.when(valid)
    def _():
        for t in range(min(depth - 1, tiles)):
            copy(t).start()

        def step(t, carry):
            @pl.when(t + depth - 1 < tiles)
            def _():
                copy(t + depth - 1).start()

            copy(t).wait()
            product(t)
            turn(lax.max(t - 1, 0))
            return carry

        lax.fori_loop(0, tiles, step, 0)
        turn(tiles - 1)

    @pl.when(jnp.logical_not(valid))
    def _():
        mine_ref[...] = jnp.zeros_like(mine_ref)
        theirs_ref[...] = jnp.zeros_like(theirs_ref)


def slot_product(base, meta, ancestor, high, low, chunks, block, after):
    cols, width = high.shape
    tile = tile_of(block, 256, 128)
    rows = width // chunks
    half = chunks // 2
    in_vmem = pl.BlockSpec(memory_space=pltpu.VMEM)
    return pl.pallas_call(
        functools.partial(slot_kernel, base, tile, len(after)),
        grid_spec=pltpu.PrefetchScalarGridSpec(
            num_scalar_prefetch=1,
            grid=(1,),
            in_specs=[ANY, in_vmem, in_vmem] + [ANY] * len(after),
            out_specs=[in_vmem, in_vmem],
            scratch_shapes=[
                pltpu.VMEM((3, tile, cols), F32),
                pltpu.VMEM((2, tile, width), F32),
                pltpu.SemaphoreType.DMA((3,)),
            ],
        ),
        out_shape=[jax.ShapeDtypeStruct((half, rows, block), F32)] * 2,
        compiler_params=PARAMS,
        cost_estimate=pl.CostEstimate(
            flops=PRODUCT_FLOPS, bytes_accessed=4 * block * cols, transcendentals=0
        ),
        name="slot_product",
    )(meta, ancestor, high, low, *after)


def place_kernel(base, fields, terms, ignored, meta_ref, *refs):
    count = len(terms)
    parts = [refs[sum(terms[:k]) : sum(terms[: k + 1])] for k in range(count)]
    outs = refs[sum(terms) + ignored :]
    rows_ref, sends = outs[0], outs[1:]
    groups = rows_ref.shape[2] // parts[0][0].shape[2]
    block = parts[0][0].shape[2]
    place = meta_ref[base + 2] // 2
    rows_ref[...] = jnp.zeros_like(rows_ref)
    for send in sends:
        send[...] = jnp.zeros_like(send)
    for k in range(count):
        at = meta_ref[base + k * fields]

        @pl.when(meta_ref[base + k * fields + 1] > 0)
        def _(k=k, at=at):
            total = parts[k][0][0]
            for term in parts[k][1:]:
                total = total + term[0]
            for g in range(groups):

                @pl.when(at == g)
                def _():
                    rows_ref[0, :, g * block : (g + 1) * block] = total

            for flip, send in enumerate(sends):

                @pl.when(at == (place ^ flip))
                def _():
                    send[...] = total


def place_slots(base, fields, meta, parts, member, members, previous, local_rows, line, exchange, after):
    rows, block = parts[0][0].shape[1:]
    terms = [len(part) for part in parts]
    arrays = [term for part in parts for term in part]
    first = pl.BlockSpec((1, rows, block), lambda i, meta_ref: (0, 0, 0))
    in_specs = [first] * len(arrays)
    aliases = {}
    if previous is not None:
        aliases = {1 + len(arrays): 0}
        arrays.append(previous)
        in_specs.append(ANY)
    arrays += after
    in_specs += [ANY] * len(after)
    ignored = len(after) + (previous is not None)
    out_specs = [pl.BlockSpec((1, rows, local_rows), lambda i, meta_ref: (member, 0, 0))]
    out_shape = [jax.ShapeDtypeStruct((members, rows, local_rows), F32)]
    if exchange:
        out_specs += [pl.BlockSpec((rows, block), lambda i, meta_ref: (0, 0))] * line
        out_shape += [jax.ShapeDtypeStruct((rows, block), F32)] * line
    return pl.pallas_call(
        functools.partial(place_kernel, base, fields, terms, ignored),
        grid_spec=pltpu.PrefetchScalarGridSpec(
            num_scalar_prefetch=1, grid=(1,), in_specs=in_specs, out_specs=out_specs
        ),
        out_shape=out_shape,
        input_output_aliases=aliases,
        compiler_params=PARAMS,
        cost_estimate=cost(1024),
        name="place_slots",
    )(meta, *arrays)


def split_kernel(core_ref, *refs):
    pieces, out = refs[:-1], refs[-1]
    half = out.shape[2]
    for at, piece in enumerate(pieces):
        for core in range(2):

            @pl.when(core_ref[0] == core)
            def _():
                out[at] = piece[:, (1 - core) * half : (2 - core) * half]


def split_halves(core, pieces):
    rows, block = pieces[0].shape
    whole = pl.BlockSpec((rows, block), lambda i, core_ref: (0, 0))
    shape = (len(pieces), rows, block // 2)
    return pl.pallas_call(
        split_kernel,
        grid_spec=pltpu.PrefetchScalarGridSpec(
            num_scalar_prefetch=1,
            grid=(1,),
            in_specs=[whole] * len(pieces),
            out_specs=pl.BlockSpec(shape, lambda i, core_ref: (0, 0, 0)),
        ),
        out_shape=jax.ShapeDtypeStruct(shape, F32),
        compiler_params=PARAMS,
        cost_estimate=cost(1024),
        name="split_halves",
    )(core.reshape(1), *pieces)


def panel_kernel(line, col_ref, *refs):
    pieces, swapped, out, whole = refs[:line], refs[line], refs[-2], refs[-1]
    rows = pieces[0].shape[0]
    half = swapped.shape[2]
    me = col_ref[0]
    core = me % 2
    for flip, piece in enumerate(pieces):
        for side in range(2):

            @pl.when(core == side)
            def _():
                first = pl.multiple_of((me ^ (2 * flip)) * rows, rows)
                whole[pl.ds(first, rows), :] = piece[:, side * half : (side + 1) * half]

        first = pl.multiple_of((me ^ (2 * flip + 1)) * rows, rows)
        whole[pl.ds(first, rows), :] = swapped[flip]
    out[0] = whole[...].T


def place_panel(col_place, pieces, swapped, member, members, previous):
    line = len(pieces)
    rows, block = pieces[0].shape
    half = block // 2
    width = 2 * line * rows
    arrays = list(pieces) + [swapped]
    in_specs = [pl.BlockSpec((rows, block), lambda i, col_ref: (0, 0))] * line
    in_specs.append(pl.BlockSpec(swapped.shape, lambda i, col_ref: (0, 0, 0)))
    aliases = {}
    if previous is not None:
        aliases = {1 + len(arrays): 0}
        arrays.append(previous)
        in_specs.append(ANY)
    return pl.pallas_call(
        functools.partial(panel_kernel, line),
        grid_spec=pltpu.PrefetchScalarGridSpec(
            num_scalar_prefetch=1,
            grid=(1,),
            in_specs=in_specs,
            out_specs=pl.BlockSpec((1, half, width), lambda i, col_ref: (member, 0, 0)),
            scratch_shapes=[pltpu.VMEM((width, half), F32)],
        ),
        out_shape=jax.ShapeDtypeStruct((members, half, width), F32),
        input_output_aliases=aliases,
        compiler_params=PARAMS,
        cost_estimate=cost(1024),
        name="place_panel",
    )(col_place.reshape(1), *arrays)


def halves_kernel(deps, first, second, *refs):
    first_out, second_out = refs[deps:]
    first_out[...] = first[...]
    second_out[...] = second[...]


def gather_rows(mine, count, after):
    half, cols = mine.shape[0] // 2, mine.shape[1]
    pieces = {}
    received = []

    def swap(value, mask):
        return lax.ppermute(value, "row", [(i, i ^ mask) for i in range(count)])

    for mask in sorted(range(1, count), key=lambda m: m.bit_count()):
        if mask.bit_count() == 1:
            whole = swap(mine, mask)
            pieces[mask] = ((whole, 0), (whole, 1))
            received.append((mask, 0, whole))
        else:
            least = mask & -mask
            most = 1 << (mask.bit_length() - 1)
            first, first_at = pieces[mask ^ most][0]
            second, second_at = pieces[mask ^ least][1]
            out = pl.BlockSpec((half, cols), lambda i: (0, 0))
            first, second = pl.pallas_call(
                functools.partial(halves_kernel, len(after)),
                grid=(1,),
                in_specs=[
                    pl.BlockSpec((half, cols), lambda i, at=first_at: (at, 0)),
                    pl.BlockSpec((half, cols), lambda i, at=second_at: (at, 0)),
                ]
                + [ANY] * len(after),
                out_specs=[out, out],
                out_shape=[jax.ShapeDtypeStruct((half, cols), F32)] * 2,
                compiler_params=PARAMS,
                cost_estimate=cost(1024),
                name="relay_halves",
            )(first, second, *after)
            first, second = swap(first, most), swap(second, least)
            pieces[mask] = ((first, 0), (second, 0))
            received.append((mask, 0, first))
            received.append((mask, half, second))
    return received


def swap_col(value, flip, count):
    return lax.ppermute(value, "col", [(c, c ^ flip) for c in range(count)])


def terms_of_sum(mine, theirs, count):
    size = theirs.shape[0] // SWAP_PARTS
    swapped = [swap_col(theirs[at : at + size], 1, count) for at in range(0, theirs.shape[0], size)]
    terms = [mine, swapped[0] if len(swapped) == 1 else jnp.concatenate(swapped)]
    flip = 2
    while flip < count:
        half = terms[-1].shape[0] // 2
        payload = sum(term[half : 2 * half] for term in terms)
        terms.append(swap_col(payload, flip, count))
        flip *= 2
    return terms


def listed_in(block_lists, blocks):
    return jnp.any(block_lists[:, :, None] == blocks[None, None, :], axis=1)


def per_device(ancestor, factor_rows, block_lists):
    members, share, local_cols = factor_rows.shape
    local_rows = ancestor.shape[0]
    row_count, col_count = lax.axis_size("row"), lax.axis_size("col")
    row_place, col_place = lax.axis_index("row"), lax.axis_index("col")
    width = share * row_count
    line = col_count // 2
    core = col_place % 2
    block = min(BS, local_rows)
    groups = local_rows // block
    unit = min(BS, local_cols)
    units = local_cols // unit
    rows_out = local_rows // col_count
    exchange = 2 * rows_out == block
    bits = col_count.bit_length() - 1

    row_blocks = (row_place * local_rows + block * lax.iota(I32, groups)) // BS
    col_blocks = (col_place * local_cols + unit * lax.iota(I32, units)) // BS
    row_listed = listed_in(block_lists, row_blocks)
    col_listed = listed_in(block_lists, col_blocks).astype(I32)
    rank = jnp.cumsum(row_listed.astype(I32), axis=1) - 1
    slots = lax.iota(I32, groups)
    chosen = row_listed[:, None, :] & (rank[:, None, :] == slots[None, :, None])
    slot_block = jnp.sum(chosen * slots[None, None, :], axis=2)
    slot_valid = jnp.any(chosen, axis=2)
    fields = 4 + units
    meta = jnp.concatenate(
        [
            slot_block[:, :, None],
            slot_valid[:, :, None].astype(I32),
            jnp.broadcast_to(col_place, (members, groups, 1)).astype(I32),
            jnp.broadcast_to(row_place, (members, groups, 1)).astype(I32),
            jnp.broadcast_to(col_listed[:, None, :], (members, groups, units)),
        ],
        axis=2,
    ).reshape(-1)

    usual = groups if groups <= 1 else groups - 1
    group_of = block_lists * BS // local_rows
    held = jnp.sum(group_of[:, :, None] == lax.iota(I32, row_count)[None, None, :], axis=1)
    fullest = jnp.max(held, axis=1)
    out_rows = width // col_count

    def slot_terms(s, k, factors, after):
        base = (s * groups + k) * fields
        mine, theirs = slot_product(base, meta, ancestor, *factors, col_count, block, after)
        return terms_of_sum(mine, theirs, col_count)

    def rest(s, factors):
        def taken():
            totals = []
            for k in range(usual, groups):
                terms = slot_terms(s, k, factors, [])
                totals.append(sum(term[0] for term in terms)[None])
            return totals

        def left():
            return [jnp.zeros((1, out_rows, block), F32) for _ in range(usual, groups)]

        if usual == groups:
            return []
        return [[total] for total in lax.cond(fullest[s] > usual, taken, left)]

    def exchange_of(placed):
        pieces = [placed[1]]
        for flip in range(1, line):
            pieces.append(swap_col(placed[1 + flip], 2 * flip, col_count))
        return pieces

    done, placed, pieces = [], [], []
    rows_all = None
    own = share_of(factor_rows, 0)
    for s in range(members):
        relay_after = [done[RELAY_AFTER][0]] if len(done) > RELAY_AFTER else []
        received = gather_rows(own, row_count, relay_after)
        following = s + 1 if s + 1 < members else None
        high, low, own = prepare(
            s * groups * fields, meta, factor_rows, own, received, width, unit, bits, following
        )
        parts = []
        others = []
        for k in range(usual):
            after = []
            for step, lag in enumerate(LAGS):
                if 0 < lag <= len(done) and step < len(done[-lag]):
                    after.append(done[-lag][step])
            if s > 0 and k == usual - 1 - PLACE_EARLY:
                after.append(placed[s - 1][-1])
            done.append(slot_terms(s, k, (high, low), after))
            parts.append(done[-1])
            if k == 0:
                others = rest(s, (high, low))
        after = pieces[s - 1][1:] if s > 0 and exchange and PLACE_WAITS else []
        placed.append(
            place_slots(
                s * groups * fields,
                fields,
                meta,
                parts + others,
                s,
                members,
                rows_all,
                local_rows,
                line,
                exchange,
                after,
            )
        )
        rows_all = placed[s][0]
        if exchange:
            pieces.append(exchange_of(placed[s]))

    panel = None
    panel_parts = []
    for s in range(members):
        if exchange:
            swapped = swap_col(split_halves(core, pieces[s]), 1, col_count)
            panel = place_panel(col_place, pieces[s], swapped, s, members, panel)
        else:
            outgoing = rows_all[s].reshape(out_rows, col_count, rows_out)
            arrived = lax.all_to_all(outgoing, "col", split_axis=1, concat_axis=0, tiled=True)
            panel_parts.append(arrived.reshape(width, rows_out).T)
    if not exchange:
        panel = jnp.stack(panel_parts)
    return panel, rows_all


def solution(mesh):
    in_specs = (P("row", "col"), P(None, "row", "col"), P())
    out_specs = (P(None, ("row", "col"), None), P(None, "col", "row"))
    return jax.shard_map(
        per_device, mesh=mesh, in_specs=in_specs, out_specs=out_specs, check_vma=False
    )
```

```python
import functools

import jax
import jax.numpy as jnp
from jax import lax
from jax.experimental import pallas as pl
from jax.experimental.pallas import tpu as pltpu
from jax.sharding import PartitionSpec as P

BS = 1280
F32 = jnp.float32
BF16 = jnp.bfloat16
I32 = jnp.int32
VMEM_LIMIT = 20 * 1024 * 1024
PARAMS = pltpu.CompilerParams(vmem_limit_bytes=VMEM_LIMIT)
LAGS = (2, 3, 4)
PRODUCT_FLOPS = int(2e9)
RELAY_AFTER = 1
ANY = pl.BlockSpec(memory_space=pl.ANY)


def tile_of(extent, wanted, step):
    best = extent
    for size in range(step, wanted + 1, step):
        if extent % size == 0:
            best = size
    return best


def cost(bytes_accessed):
    return pl.CostEstimate(flops=0, bytes_accessed=bytes_accessed, transcendentals=0)


def copy_kernel(source, target):
    target[...] = source[0]


def share_of(factor_rows, member):
    share, cols = factor_rows.shape[1:]
    return pl.pallas_call(
        copy_kernel,
        grid=(1,),
        in_specs=[pl.BlockSpec((1, share, cols), lambda i: (member, 0, 0))],
        out_specs=pl.BlockSpec((share, cols), lambda i: (0, 0)),
        out_shape=jax.ShapeDtypeStruct((share, cols), F32),
        compiler_params=PARAMS,
        cost_estimate=cost(1024),
        name="own_share",
    )(factor_rows)


def prep_kernel(places, share, following, base, units, bits, meta_ref, *refs):
    pieces = refs[: len(places)]
    rest = refs[len(places) :]
    if following:
        next_in, high_ref, low_ref, next_out, whole = rest
        next_out[...] = next_in[0]
    else:
        high_ref, low_ref, whole = rest
    me = meta_ref[base + 2]
    row = meta_ref[base + 3]
    step = pl.program_id(0)
    rows = whole.shape[0] >> bits
    for (mask, offset), piece in zip(places, pieces):
        first = (row ^ mask) * share + offset
        for at in range(0, piece.shape[0], rows):
            flip = ((first + at) // rows) ^ me
            turned_flip = sum(((flip >> bit) & 1) << (bits - 1 - bit) for bit in range(bits))
            whole[pl.ds(pl.multiple_of(turned_flip * rows, rows), rows), :] = piece[at : at + rows, :]
    scale = jnp.where(meta_ref[base + 4 + step] > 0, -1.0, 0.0).astype(F32)
    turned = whole[...].T * scale
    high = turned.astype(BF16)
    high_ref[...] = high
    low_ref[...] = (turned - high.astype(F32)).astype(BF16)


def prepare(base, meta, factor_rows, own, received, width, unit, bits, following):
    share, cols = own.shape
    units = cols // unit
    places = [(0, 0)] + [(mask, offset) for mask, offset, _ in received]
    arrays = [own] + [piece for _, _, piece in received]
    in_specs = [pl.BlockSpec((piece.shape[0], unit), lambda i, m: (0, i)) for piece in arrays]
    out_specs = [pl.BlockSpec((unit, width), lambda i, m: (i, 0))] * 2
    out_shape = [jax.ShapeDtypeStruct((cols, width), BF16)] * 2
    if following is not None:
        arrays.append(factor_rows)
        in_specs.append(pl.BlockSpec((1, share, unit), lambda i, m: (following, 0, i)))
        out_specs.append(pl.BlockSpec((share, unit), lambda i, m: (0, i)))
        out_shape.append(jax.ShapeDtypeStruct((share, cols), F32))
    outs = pl.pallas_call(
        functools.partial(prep_kernel, places, share, following is not None, base, units, bits),
        grid_spec=pltpu.PrefetchScalarGridSpec(
            num_scalar_prefetch=1,
            grid=(units,),
            in_specs=in_specs,
            out_specs=out_specs,
            scratch_shapes=[pltpu.VMEM((width, unit), F32)],
        ),
        out_shape=out_shape,
        compiler_params=PARAMS,
        cost_estimate=cost(1024),
        name="prepare_factor",
    )(meta, *arrays)
    return outs if following is not None else (*outs, None)


def slot_kernel(base, tile, deps, meta_ref, a_ref, high_ref, low_ref, *refs):
    mine_ref, theirs_ref, buffer, total, arrived = refs[deps:]
    half, rows, block = mine_ref.shape
    tiles = block // tile
    depth = buffer.shape[0]
    first = meta_ref[base] * block

    def copy(t):
        source = a_ref.at[pl.ds(pl.multiple_of(first + t * tile, tile), tile), :]
        slot = lax.rem(t, depth)
        return pltpu.make_async_copy(source, buffer.at[slot], arrived.at[slot])

    def turn(t):
        turned = total[lax.rem(t, 2)].T
        columns = pl.ds(pl.multiple_of(t * tile, tile), tile)
        mine_ref[:, :, columns] = turned[: half * rows].reshape(half, rows, tile)
        theirs_ref[:, :, columns] = turned[half * rows :].reshape(half, rows, tile)

    def product(t):
        a = buffer[lax.rem(t, depth)]
        a_high = a.astype(BF16)
        a_low = (a - a_high.astype(F32)).astype(BF16)
        dot = functools.partial(jnp.dot, preferred_element_type=F32)
        total[lax.rem(t, 2)] = (
            dot(a_high, high_ref[...]) + dot(a_high, low_ref[...]) + dot(a_low, high_ref[...])
        )

    valid = meta_ref[base + 1] > 0

    @pl.when(valid)
    def _():
        for t in range(min(depth - 1, tiles)):
            copy(t).start()

        def step(t, carry):
            @pl.when(t + depth - 1 < tiles)
            def _():
                copy(t + depth - 1).start()

            copy(t).wait()
            product(t)
            turn(lax.max(t - 1, 0))
            return carry

        lax.fori_loop(0, tiles, step, 0)
        turn(tiles - 1)

    @pl.when(jnp.logical_not(valid))
    def _():
        mine_ref[...] = jnp.zeros_like(mine_ref)
        theirs_ref[...] = jnp.zeros_like(theirs_ref)


def slot_product(base, meta, ancestor, high, low, chunks, block, after):
    cols, width = high.shape
    tile = tile_of(block, 256, 128)
    rows = width // chunks
    half = chunks // 2
    in_vmem = pl.BlockSpec(memory_space=pltpu.VMEM)
    return pl.pallas_call(
        functools.partial(slot_kernel, base, tile, len(after)),
        grid_spec=pltpu.PrefetchScalarGridSpec(
            num_scalar_prefetch=1,
            grid=(1,),
            in_specs=[ANY, in_vmem, in_vmem] + [ANY] * len(after),
            out_specs=[in_vmem, in_vmem],
            scratch_shapes=[
                pltpu.VMEM((3, tile, cols), F32),
                pltpu.VMEM((2, tile, width), F32),
                pltpu.SemaphoreType.DMA((3,)),
            ],
        ),
        out_shape=[jax.ShapeDtypeStruct((half, rows, block), F32)] * 2,
        compiler_params=PARAMS,
        cost_estimate=pl.CostEstimate(
            flops=PRODUCT_FLOPS, bytes_accessed=4 * block * cols, transcendentals=0
        ),
        name="slot_product",
    )(meta, ancestor, high, low, *after)


def place_kernel(base, fields, terms, ignored, meta_ref, *refs):
    count = len(terms)
    parts = [refs[sum(terms[:k]) : sum(terms[: k + 1])] for k in range(count)]
    outs = refs[sum(terms) + ignored :]
    rows_ref, sends = outs[0], outs[1:]
    groups = rows_ref.shape[2] // parts[0][0].shape[2]
    block = parts[0][0].shape[2]
    place = meta_ref[base + 2] // 2
    rows_ref[...] = jnp.zeros_like(rows_ref)
    for send in sends:
        send[...] = jnp.zeros_like(send)
    for k in range(count):
        at = meta_ref[base + k * fields]

        @pl.when(meta_ref[base + k * fields + 1] > 0)
        def _(k=k, at=at):
            total = parts[k][0][0]
            for term in parts[k][1:]:
                total = total + term[0]
            for g in range(groups):

                @pl.when(at == g)
                def _():
                    rows_ref[0, :, g * block : (g + 1) * block] = total

            for flip, send in enumerate(sends):

                @pl.when(at == (place ^ flip))
                def _():
                    send[...] = total


def place_slots(base, fields, meta, parts, member, members, previous, local_rows, line, exchange, after):
    rows, block = parts[0][0].shape[1:]
    terms = [len(part) for part in parts]
    arrays = [term for part in parts for term in part]
    first = pl.BlockSpec((1, rows, block), lambda i, meta_ref: (0, 0, 0))
    in_specs = [first] * len(arrays)
    aliases = {}
    if previous is not None:
        aliases = {1 + len(arrays): 0}
        arrays.append(previous)
        in_specs.append(ANY)
    arrays += after
    in_specs += [ANY] * len(after)
    ignored = len(after) + (previous is not None)
    out_specs = [pl.BlockSpec((1, rows, local_rows), lambda i, meta_ref: (member, 0, 0))]
    out_shape = [jax.ShapeDtypeStruct((members, rows, local_rows), F32)]
    if exchange:
        out_specs += [pl.BlockSpec((rows, block), lambda i, meta_ref: (0, 0))] * line
        out_shape += [jax.ShapeDtypeStruct((rows, block), F32)] * line
    return pl.pallas_call(
        functools.partial(place_kernel, base, fields, terms, ignored),
        grid_spec=pltpu.PrefetchScalarGridSpec(
            num_scalar_prefetch=1, grid=(1,), in_specs=in_specs, out_specs=out_specs
        ),
        out_shape=out_shape,
        input_output_aliases=aliases,
        compiler_params=PARAMS,
        cost_estimate=cost(1024),
        name="place_slots",
    )(meta, *arrays)


def split_kernel(core_ref, *refs):
    pieces, out = refs[:-1], refs[-1]
    half = out.shape[2]
    for at, piece in enumerate(pieces):
        for core in range(2):

            @pl.when(core_ref[0] == core)
            def _():
                out[at] = piece[:, (1 - core) * half : (2 - core) * half]


def split_halves(core, pieces):
    rows, block = pieces[0].shape
    whole = pl.BlockSpec((rows, block), lambda i, core_ref: (0, 0))
    shape = (len(pieces), rows, block // 2)
    return pl.pallas_call(
        split_kernel,
        grid_spec=pltpu.PrefetchScalarGridSpec(
            num_scalar_prefetch=1,
            grid=(1,),
            in_specs=[whole] * len(pieces),
            out_specs=pl.BlockSpec(shape, lambda i, core_ref: (0, 0, 0)),
        ),
        out_shape=jax.ShapeDtypeStruct(shape, F32),
        compiler_params=PARAMS,
        cost_estimate=cost(1024),
        name="split_halves",
    )(core.reshape(1), *pieces)


def panel_kernel(line, col_ref, *refs):
    pieces, swapped, out, whole = refs[:line], refs[line], refs[-2], refs[-1]
    rows = pieces[0].shape[0]
    half = swapped.shape[2]
    me = col_ref[0]
    core = me % 2
    for flip, piece in enumerate(pieces):
        for side in range(2):

            @pl.when(core == side)
            def _():
                first = pl.multiple_of((me ^ (2 * flip)) * rows, rows)
                whole[pl.ds(first, rows), :] = piece[:, side * half : (side + 1) * half]

        first = pl.multiple_of((me ^ (2 * flip + 1)) * rows, rows)
        whole[pl.ds(first, rows), :] = swapped[flip]
    out[0] = whole[...].T


def place_panel(col_place, pieces, swapped, member, members, previous):
    line = len(pieces)
    rows, block = pieces[0].shape
    half = block // 2
    width = 2 * line * rows
    arrays = list(pieces) + [swapped]
    in_specs = [pl.BlockSpec((rows, block), lambda i, col_ref: (0, 0))] * line
    in_specs.append(pl.BlockSpec(swapped.shape, lambda i, col_ref: (0, 0, 0)))
    aliases = {}
    if previous is not None:
        aliases = {1 + len(arrays): 0}
        arrays.append(previous)
        in_specs.append(ANY)
    return pl.pallas_call(
        functools.partial(panel_kernel, line),
        grid_spec=pltpu.PrefetchScalarGridSpec(
            num_scalar_prefetch=1,
            grid=(1,),
            in_specs=in_specs,
            out_specs=pl.BlockSpec((1, half, width), lambda i, col_ref: (member, 0, 0)),
            scratch_shapes=[pltpu.VMEM((width, half), F32)],
        ),
        out_shape=jax.ShapeDtypeStruct((members, half, width), F32),
        input_output_aliases=aliases,
        compiler_params=PARAMS,
        cost_estimate=cost(1024),
        name="place_panel",
    )(col_place.reshape(1), *arrays)


def halves_kernel(deps, first, second, *refs):
    first_out, second_out = refs[deps:]
    first_out[...] = first[...]
    second_out[...] = second[...]


def gather_rows(mine, count, after):
    half, cols = mine.shape[0] // 2, mine.shape[1]
    pieces = {}
    received = []

    def swap(value, mask):
        return lax.ppermute(value, "row", [(i, i ^ mask) for i in range(count)])

    for mask in sorted(range(1, count), key=lambda m: m.bit_count()):
        if mask.bit_count() == 1:
            whole = swap(mine, mask)
            pieces[mask] = ((whole, 0), (whole, 1))
            received.append((mask, 0, whole))
        else:
            least = mask & -mask
            most = 1 << (mask.bit_length() - 1)
            first, first_at = pieces[mask ^ most][0]
            second, second_at = pieces[mask ^ least][1]
            out = pl.BlockSpec((half, cols), lambda i: (0, 0))
            first, second = pl.pallas_call(
                functools.partial(halves_kernel, len(after)),
                grid=(1,),
                in_specs=[
                    pl.BlockSpec((half, cols), lambda i, at=first_at: (at, 0)),
                    pl.BlockSpec((half, cols), lambda i, at=second_at: (at, 0)),
                ]
                + [ANY] * len(after),
                out_specs=[out, out],
                out_shape=[jax.ShapeDtypeStruct((half, cols), F32)] * 2,
                compiler_params=PARAMS,
                cost_estimate=cost(1024),
                name="relay_halves",
            )(first, second, *after)
            first, second = swap(first, most), swap(second, least)
            pieces[mask] = ((first, 0), (second, 0))
            received.append((mask, 0, first))
            received.append((mask, half, second))
    return received


def swap_col(value, flip, count):
    return lax.ppermute(value, "col", [(c, c ^ flip) for c in range(count)])


def halved_sum(mine, theirs, count):
    arrived = [swap_col(theirs, 1, count)]
    terms = [mine, arrived[0]]
    flip = 2
    while flip < count:
        half = terms[-1].shape[0] // 2
        payload = sum(term[half : 2 * half] for term in terms)
        arrived.append(swap_col(payload, flip, count))
        terms.append(arrived[-1])
        flip *= 2
    return arrived, [sum(term[:1] for term in terms[:-1]), terms[-1][:1]]


def listed_in(block_lists, blocks):
    return jnp.any(block_lists[:, :, None] == blocks[None, None, :], axis=1)


def per_device(ancestor, factor_rows, block_lists):
    members, share, local_cols = factor_rows.shape
    local_rows = ancestor.shape[0]
    row_count, col_count = lax.axis_size("row"), lax.axis_size("col")
    row_place, col_place = lax.axis_index("row"), lax.axis_index("col")
    width = share * row_count
    line = col_count // 2
    core = col_place % 2
    block = min(BS, local_rows)
    groups = local_rows // block
    unit = min(BS, local_cols)
    units = local_cols // unit
    rows_out = local_rows // col_count
    exchange = 2 * rows_out == block
    bits = col_count.bit_length() - 1

    row_blocks = (row_place * local_rows + block * lax.iota(I32, groups)) // BS
    col_blocks = (col_place * local_cols + unit * lax.iota(I32, units)) // BS
    row_listed = listed_in(block_lists, row_blocks)
    col_listed = listed_in(block_lists, col_blocks).astype(I32)
    rank = jnp.cumsum(row_listed.astype(I32), axis=1) - 1
    slots = lax.iota(I32, groups)
    chosen = row_listed[:, None, :] & (rank[:, None, :] == slots[None, :, None])
    slot_block = jnp.sum(chosen * slots[None, None, :], axis=2)
    slot_valid = jnp.any(chosen, axis=2)
    fields = 4 + units
    meta = jnp.concatenate(
        [
            slot_block[:, :, None],
            slot_valid[:, :, None].astype(I32),
            jnp.broadcast_to(col_place, (members, groups, 1)).astype(I32),
            jnp.broadcast_to(row_place, (members, groups, 1)).astype(I32),
            jnp.broadcast_to(col_listed[:, None, :], (members, groups, units)),
        ],
        axis=2,
    ).reshape(-1)

    usual = groups if groups <= 1 else groups - 1
    group_of = block_lists * BS // local_rows
    held = jnp.sum(group_of[:, :, None] == lax.iota(I32, row_count)[None, None, :], axis=1)
    fullest = jnp.max(held, axis=1)
    out_rows = width // col_count

    def slot_sum(s, k, factors, after):
        base = (s * groups + k) * fields
        mine, theirs = slot_product(base, meta, ancestor, *factors, col_count, block, after)
        return halved_sum(mine, theirs, col_count)

    def rest(s, factors):
        def taken():
            return [sum(slot_sum(s, k, factors, [])[1]) for k in range(usual, groups)]

        def left():
            return [jnp.zeros((1, out_rows, block), F32) for _ in range(usual, groups)]

        if usual == groups:
            return []
        return [[total] for total in lax.cond(fullest[s] > usual, taken, left)]

    def exchange_of(placed):
        pieces = [placed[1]]
        for flip in range(1, line):
            pieces.append(swap_col(placed[1 + flip], 2 * flip, col_count))
        return pieces

    done, parts, others, placed, pieces = [], [], [], [], []

    def place(s):
        placed.append(
            place_slots(
                s * groups * fields,
                fields,
                meta,
                parts[s] + others[s],
                s,
                members,
                placed[s - 1][0] if s > 0 else None,
                local_rows,
                line,
                exchange,
                [],
            )
        )
        if exchange:
            pieces.append(exchange_of(placed[s]))

    own = share_of(factor_rows, 0)
    for s in range(members):
        relay_after = [done[RELAY_AFTER][0]] if len(done) > RELAY_AFTER else []
        received = gather_rows(own, row_count, relay_after)
        following = s + 1 if s + 1 < members else None
        high, low, own = prepare(
            s * groups * fields, meta, factor_rows, own, received, width, unit, bits, following
        )
        parts.append([])
        for k in range(usual):
            after = []
            for step, lag in enumerate(LAGS):
                if 0 < lag <= len(done) and step < len(done[-lag]):
                    after.append(done[-lag][step])
            if s > 0 and k == usual - 1:
                place(s - 1)
            arrived, terms = slot_sum(s, k, (high, low), after)
            done.append(arrived)
            parts[s].append(terms)
            if k == 0:
                others.append(rest(s, (high, low)))
    place(members - 1)
    rows_all = placed[-1][0]

    panel = None
    panel_parts = []
    for s in range(members):
        if exchange:
            swapped = swap_col(split_halves(core, pieces[s]), 1, col_count)
            panel = place_panel(col_place, pieces[s], swapped, s, members, panel)
        else:
            outgoing = rows_all[s].reshape(out_rows, col_count, rows_out)
            arrived = lax.all_to_all(outgoing, "col", split_axis=1, concat_axis=0, tiled=True)
            panel_parts.append(arrived.reshape(width, rows_out).T)
    if not exchange:
        panel = jnp.stack(panel_parts)
    return panel, rows_all


def solution(mesh):
    in_specs = (P("row", "col"), P(None, "row", "col"), P())
    out_specs = (P(None, ("row", "col"), None), P(None, "col", "row"))
    return jax.shard_map(
        per_device, mesh=mesh, in_specs=in_specs, out_specs=out_specs, check_vma=False
    )
```

```python
import functools

import jax
import jax.numpy as jnp
from jax import lax
from jax.experimental import pallas as pl
from jax.experimental.pallas import tpu as pltpu
from jax.sharding import PartitionSpec as P

BS = 1280
F32 = jnp.float32
BF16 = jnp.bfloat16
I32 = jnp.int32
VMEM_LIMIT = 20 * 1024 * 1024
PARAMS = pltpu.CompilerParams(vmem_limit_bytes=VMEM_LIMIT)
LAGS = (2, 3, 5)
PRODUCT_FLOPS = 0
RELAY_AT = 2
ANY = pl.BlockSpec(memory_space=pl.ANY)


def tile_of(extent, wanted, step):
    best = extent
    for size in range(step, wanted + 1, step):
        if extent % size == 0:
            best = size
    return best


def cost(bytes_accessed):
    return pl.CostEstimate(flops=0, bytes_accessed=bytes_accessed, transcendentals=0)


def copy_kernel(source, target):
    target[...] = source[0]


def share_of(factor_rows, member):
    share, cols = factor_rows.shape[1:]
    return pl.pallas_call(
        copy_kernel,
        grid=(1,),
        in_specs=[pl.BlockSpec((1, share, cols), lambda i: (member, 0, 0))],
        out_specs=pl.BlockSpec((share, cols), lambda i: (0, 0)),
        out_shape=jax.ShapeDtypeStruct((share, cols), F32),
        compiler_params=PARAMS,
        cost_estimate=cost(1024),
        name="own_share",
    )(factor_rows)


def prep_kernel(places, share, following, base, units, bits, meta_ref, *refs):
    pieces = refs[: len(places)]
    rest = refs[len(places) :]
    if following:
        next_in, high_ref, low_ref, next_out, whole = rest
        next_out[...] = next_in[0]
    else:
        high_ref, low_ref, whole = rest
    me = meta_ref[base + 2]
    row = meta_ref[base + 3]
    step = pl.program_id(0)
    rows = whole.shape[0] >> bits
    for (mask, offset), piece in zip(places, pieces):
        first = (row ^ mask) * share + offset
        for at in range(0, piece.shape[0], rows):
            flip = ((first + at) // rows) ^ me
            turned_flip = sum(((flip >> bit) & 1) << (bits - 1 - bit) for bit in range(bits))
            whole[pl.ds(pl.multiple_of(turned_flip * rows, rows), rows), :] = piece[at : at + rows, :]
    scale = jnp.where(meta_ref[base + 4 + step] > 0, -1.0, 0.0).astype(F32)
    turned = whole[...].T * scale
    high = turned.astype(BF16)
    high_ref[...] = high
    low_ref[...] = (turned - high.astype(F32)).astype(BF16)


def prepare(base, meta, factor_rows, own, received, width, unit, bits, following):
    share, cols = own.shape
    units = cols // unit
    places = [(0, 0)] + [(mask, offset) for mask, offset, _ in received]
    arrays = [own] + [piece for _, _, piece in received]
    in_specs = [pl.BlockSpec((piece.shape[0], unit), lambda i, m: (0, i)) for piece in arrays]
    out_specs = [pl.BlockSpec((unit, width), lambda i, m: (i, 0))] * 2
    out_shape = [jax.ShapeDtypeStruct((cols, width), BF16)] * 2
    if following is not None:
        arrays.append(factor_rows)
        in_specs.append(pl.BlockSpec((1, share, unit), lambda i, m: (following, 0, i)))
        out_specs.append(pl.BlockSpec((share, unit), lambda i, m: (0, i)))
        out_shape.append(jax.ShapeDtypeStruct((share, cols), F32))
    outs = pl.pallas_call(
        functools.partial(prep_kernel, places, share, following is not None, base, units, bits),
        grid_spec=pltpu.PrefetchScalarGridSpec(
            num_scalar_prefetch=1,
            grid=(units,),
            in_specs=in_specs,
            out_specs=out_specs,
            scratch_shapes=[pltpu.VMEM((width, unit), F32)],
        ),
        out_shape=out_shape,
        compiler_params=PARAMS,
        cost_estimate=cost(1024),
        name="prepare_factor",
    )(meta, *arrays)
    return outs if following is not None else (*outs, None)


def slot_kernel(base, tile, deps, meta_ref, a_ref, high_ref, low_ref, *refs):
    mine_ref, theirs_ref, buffer, total, arrived = refs[deps:]
    half, rows, block = mine_ref.shape
    tiles = block // tile
    depth = buffer.shape[0]
    first = meta_ref[base] * block

    def copy(t):
        source = a_ref.at[pl.ds(pl.multiple_of(first + t * tile, tile), tile), :]
        slot = lax.rem(t, depth)
        return pltpu.make_async_copy(source, buffer.at[slot], arrived.at[slot])

    def turn(t):
        turned = total[lax.rem(t, 2)].T
        columns = pl.ds(pl.multiple_of(t * tile, tile), tile)
        mine_ref[:, :, columns] = turned[: half * rows].reshape(half, rows, tile)
        theirs_ref[:, :, columns] = turned[half * rows :].reshape(half, rows, tile)

    def product(t):
        a = buffer[lax.rem(t, depth)]
        a_high = a.astype(BF16)
        a_low = (a - a_high.astype(F32)).astype(BF16)
        dot = functools.partial(jnp.dot, preferred_element_type=F32)
        total[lax.rem(t, 2)] = (
            dot(a_high, high_ref[...]) + dot(a_high, low_ref[...]) + dot(a_low, high_ref[...])
        )

    valid = meta_ref[base + 1] > 0

    @pl.when(valid)
    def _():
        for t in range(min(depth - 1, tiles)):
            copy(t).start()

        def step(t, carry):
            @pl.when(t + depth - 1 < tiles)
            def _():
                copy(t + depth - 1).start()

            copy(t).wait()
            product(t)
            turn(lax.max(t - 1, 0))
            return carry

        lax.fori_loop(0, tiles, step, 0)
        turn(tiles - 1)

    @pl.when(jnp.logical_not(valid))
    def _():
        mine_ref[...] = jnp.zeros_like(mine_ref)
        theirs_ref[...] = jnp.zeros_like(theirs_ref)


def slot_product(base, meta, ancestor, high, low, chunks, block, after):
    cols, width = high.shape
    tile = tile_of(block, 256, 128)
    rows = width // chunks
    half = chunks // 2
    in_vmem = pl.BlockSpec(memory_space=pltpu.VMEM)
    return pl.pallas_call(
        functools.partial(slot_kernel, base, tile, len(after)),
        grid_spec=pltpu.PrefetchScalarGridSpec(
            num_scalar_prefetch=1,
            grid=(1,),
            in_specs=[ANY, in_vmem, in_vmem] + [ANY] * len(after),
            out_specs=[in_vmem, in_vmem],
            scratch_shapes=[
                pltpu.VMEM((3, tile, cols), F32),
                pltpu.VMEM((2, tile, width), F32),
                pltpu.SemaphoreType.DMA((3,)),
            ],
        ),
        out_shape=[jax.ShapeDtypeStruct((half, rows, block), F32)] * 2,
        compiler_params=PARAMS,
        cost_estimate=pl.CostEstimate(
            flops=PRODUCT_FLOPS, bytes_accessed=4 * block * cols, transcendentals=0
        ),
        name="slot_product",
    )(meta, ancestor, high, low, *after)


def place_kernel(base, fields, terms, ignored, meta_ref, *refs):
    count = len(terms)
    parts = [refs[sum(terms[:k]) : sum(terms[: k + 1])] for k in range(count)]
    outs = refs[sum(terms) + ignored :]
    rows_ref, sends = outs[0], outs[1:]
    groups = rows_ref.shape[2] // parts[0][0].shape[2]
    block = parts[0][0].shape[2]
    place = meta_ref[base + 2] // 2
    rows_ref[...] = jnp.zeros_like(rows_ref)
    for send in sends:
        send[...] = jnp.zeros_like(send)
    for k in range(count):
        at = meta_ref[base + k * fields]

        @pl.when(meta_ref[base + k * fields + 1] > 0)
        def _(k=k, at=at):
            total = parts[k][0][0]
            for term in parts[k][1:]:
                total = total + term[0]
            for g in range(groups):

                @pl.when(at == g)
                def _():
                    rows_ref[0, :, g * block : (g + 1) * block] = total

            for flip, send in enumerate(sends):

                @pl.when(at == (place ^ flip))
                def _():
                    send[...] = total


def place_slots(base, fields, meta, parts, member, members, previous, local_rows, line, exchange, after):
    rows, block = parts[0][0].shape[1:]
    terms = [len(part) for part in parts]
    arrays = [term for part in parts for term in part]
    first = pl.BlockSpec((1, rows, block), lambda i, meta_ref: (0, 0, 0))
    in_specs = [first] * len(arrays)
    aliases = {}
    if previous is not None:
        aliases = {1 + len(arrays): 0}
        arrays.append(previous)
        in_specs.append(ANY)
    arrays += after
    in_specs += [ANY] * len(after)
    ignored = len(after) + (previous is not None)
    out_specs = [pl.BlockSpec((1, rows, local_rows), lambda i, meta_ref: (member, 0, 0))]
    out_shape = [jax.ShapeDtypeStruct((members, rows, local_rows), F32)]
    if exchange:
        out_specs += [pl.BlockSpec((rows, block), lambda i, meta_ref: (0, 0))] * line
        out_shape += [jax.ShapeDtypeStruct((rows, block), F32)] * line
    return pl.pallas_call(
        functools.partial(place_kernel, base, fields, terms, ignored),
        grid_spec=pltpu.PrefetchScalarGridSpec(
            num_scalar_prefetch=1, grid=(1,), in_specs=in_specs, out_specs=out_specs
        ),
        out_shape=out_shape,
        input_output_aliases=aliases,
        compiler_params=PARAMS,
        cost_estimate=cost(1024),
        name="place_slots",
    )(meta, *arrays)


def split_kernel(core_ref, *refs):
    pieces, out = refs[:-1], refs[-1]
    half = out.shape[2]
    for at, piece in enumerate(pieces):
        for core in range(2):

            @pl.when(core_ref[0] == core)
            def _():
                out[at] = piece[:, (1 - core) * half : (2 - core) * half]


def split_halves(core, pieces):
    rows, block = pieces[0].shape
    whole = pl.BlockSpec((rows, block), lambda i, core_ref: (0, 0))
    shape = (len(pieces), rows, block // 2)
    return pl.pallas_call(
        split_kernel,
        grid_spec=pltpu.PrefetchScalarGridSpec(
            num_scalar_prefetch=1,
            grid=(1,),
            in_specs=[whole] * len(pieces),
            out_specs=pl.BlockSpec(shape, lambda i, core_ref: (0, 0, 0)),
        ),
        out_shape=jax.ShapeDtypeStruct(shape, F32),
        compiler_params=PARAMS,
        cost_estimate=cost(1024),
        name="split_halves",
    )(core.reshape(1), *pieces)


def panel_kernel(line, col_ref, *refs):
    pieces, swapped, out, whole = refs[:line], refs[line], refs[-2], refs[-1]
    rows = pieces[0].shape[0]
    half = swapped.shape[2]
    me = col_ref[0]
    core = me % 2
    for flip, piece in enumerate(pieces):
        for side in range(2):

            @pl.when(core == side)
            def _():
                first = pl.multiple_of((me ^ (2 * flip)) * rows, rows)
                whole[pl.ds(first, rows), :] = piece[:, side * half : (side + 1) * half]

        first = pl.multiple_of((me ^ (2 * flip + 1)) * rows, rows)
        whole[pl.ds(first, rows), :] = swapped[flip]
    out[0] = whole[...].T


def place_panel(col_place, pieces, swapped, member, members, previous):
    line = len(pieces)
    rows, block = pieces[0].shape
    half = block // 2
    width = 2 * line * rows
    arrays = list(pieces) + [swapped]
    in_specs = [pl.BlockSpec((rows, block), lambda i, col_ref: (0, 0))] * line
    in_specs.append(pl.BlockSpec(swapped.shape, lambda i, col_ref: (0, 0, 0)))
    aliases = {}
    if previous is not None:
        aliases = {1 + len(arrays): 0}
        arrays.append(previous)
        in_specs.append(ANY)
    return pl.pallas_call(
        functools.partial(panel_kernel, line),
        grid_spec=pltpu.PrefetchScalarGridSpec(
            num_scalar_prefetch=1,
            grid=(1,),
            in_specs=in_specs,
            out_specs=pl.BlockSpec((1, half, width), lambda i, col_ref: (member, 0, 0)),
            scratch_shapes=[pltpu.VMEM((width, half), F32)],
        ),
        out_shape=jax.ShapeDtypeStruct((members, half, width), F32),
        input_output_aliases=aliases,
        compiler_params=PARAMS,
        cost_estimate=cost(1024),
        name="place_panel",
    )(col_place.reshape(1), *arrays)


def halves_kernel(deps, first, second, *refs):
    first_out, second_out = refs[deps:]
    first_out[...] = first[...]
    second_out[...] = second[...]


def gather_rows(mine, count, after):
    half, cols = mine.shape[0] // 2, mine.shape[1]
    pieces = {}
    received, relayed = [], []

    def swap(value, mask):
        return lax.ppermute(value, "row", [(i, i ^ mask) for i in range(count)])

    for mask in sorted(range(1, count), key=lambda m: m.bit_count()):
        if mask.bit_count() == 1:
            whole = swap(mine, mask)
            pieces[mask] = ((whole, 0), (whole, 1))
            received.append((mask, 0, whole))
        else:
            least = mask & -mask
            most = 1 << (mask.bit_length() - 1)
            first, first_at = pieces[mask ^ most][0]
            second, second_at = pieces[mask ^ least][1]
            out = pl.BlockSpec((half, cols), lambda i: (0, 0))
            first, second = pl.pallas_call(
                functools.partial(halves_kernel, len(after)),
                grid=(1,),
                in_specs=[
                    pl.BlockSpec((half, cols), lambda i, at=first_at: (at, 0)),
                    pl.BlockSpec((half, cols), lambda i, at=second_at: (at, 0)),
                ]
                + [ANY] * len(after),
                out_specs=[out, out],
                out_shape=[jax.ShapeDtypeStruct((half, cols), F32)] * 2,
                compiler_params=PARAMS,
                cost_estimate=cost(1024),
                name="relay_halves",
            )(first, second, *after)
            relayed += [first, second]
            first, second = swap(first, most), swap(second, least)
            pieces[mask] = ((first, 0), (second, 0))
            received.append((mask, 0, first))
            received.append((mask, half, second))
    return received, relayed


def swap_col(value, flip, count):
    return lax.ppermute(value, "col", [(c, c ^ flip) for c in range(count)])


def halved_sum(mine, theirs, count):
    arrived = [swap_col(theirs, 1, count)]
    terms = [mine, arrived[0]]
    flip = 2
    while flip < count:
        half = terms[-1].shape[0] // 2
        payload = sum(term[half : 2 * half] for term in terms)
        arrived.append(swap_col(payload, flip, count))
        terms.append(arrived[-1])
        flip *= 2
    return arrived, [sum(term[:1] for term in terms[:-1]), terms[-1][:1]]


def listed_in(block_lists, blocks):
    return jnp.any(block_lists[:, :, None] == blocks[None, None, :], axis=1)


def per_device(ancestor, factor_rows, block_lists):
    members, share, local_cols = factor_rows.shape
    local_rows = ancestor.shape[0]
    row_count, col_count = lax.axis_size("row"), lax.axis_size("col")
    row_place, col_place = lax.axis_index("row"), lax.axis_index("col")
    width = share * row_count
    line = col_count // 2
    core = col_place % 2
    block = min(BS, local_rows)
    groups = local_rows // block
    unit = min(BS, local_cols)
    units = local_cols // unit
    rows_out = local_rows // col_count
    exchange = 2 * rows_out == block
    bits = col_count.bit_length() - 1

    row_blocks = (row_place * local_rows + block * lax.iota(I32, groups)) // BS
    col_blocks = (col_place * local_cols + unit * lax.iota(I32, units)) // BS
    row_listed = listed_in(block_lists, row_blocks)
    col_listed = listed_in(block_lists, col_blocks).astype(I32)
    rank = jnp.cumsum(row_listed.astype(I32), axis=1) - 1
    slots = lax.iota(I32, groups)
    chosen = row_listed[:, None, :] & (rank[:, None, :] == slots[None, :, None])
    slot_block = jnp.sum(chosen * slots[None, None, :], axis=2)
    slot_valid = jnp.any(chosen, axis=2)
    fields = 4 + units
    meta = jnp.concatenate(
        [
            slot_block[:, :, None],
            slot_valid[:, :, None].astype(I32),
            jnp.broadcast_to(col_place, (members, groups, 1)).astype(I32),
            jnp.broadcast_to(row_place, (members, groups, 1)).astype(I32),
            jnp.broadcast_to(col_listed[:, None, :], (members, groups, units)),
        ],
        axis=2,
    ).reshape(-1)

    usual = groups if groups <= 1 else groups - 1
    group_of = block_lists * BS // local_rows
    held = jnp.sum(group_of[:, :, None] == lax.iota(I32, row_count)[None, None, :], axis=1)
    fullest = jnp.max(held, axis=1)
    out_rows = width // col_count

    def slot_sum(s, k, factors, after):
        base = (s * groups + k) * fields
        mine, theirs = slot_product(base, meta, ancestor, *factors, col_count, block, after)
        return halved_sum(mine, theirs, col_count)

    def rest(s, factors):
        def taken():
            return [sum(slot_sum(s, k, factors, [])[1]) for k in range(usual, groups)]

        def left():
            return [jnp.zeros((1, out_rows, block), F32) for _ in range(usual, groups)]

        if usual == groups:
            return []
        return [[total] for total in lax.cond(fullest[s] > usual, taken, left)]

    def exchange_of(placed):
        pieces = [placed[1]]
        for flip in range(1, line):
            pieces.append(swap_col(placed[1 + flip], 2 * flip, col_count))
        return pieces

    done, parts, others, placed, pieces = [], [], [], [], []

    def place(s):
        placed.append(
            place_slots(
                s * groups * fields,
                fields,
                meta,
                parts[s] + others[s],
                s,
                members,
                placed[s - 1][0] if s > 0 else None,
                local_rows,
                line,
                exchange,
                [],
            )
        )
        if exchange:
            pieces.append(exchange_of(placed[s]))

    own = share_of(factor_rows, 0)
    received, relayed = gather_rows(own, row_count, [])
    for s in range(members):
        following = s + 1 if s + 1 < members else None
        high, low, own = prepare(
            s * groups * fields, meta, factor_rows, own, received, width, unit, bits, following
        )
        parts.append([])
        for k in range(usual):
            after = []
            for step, lag in enumerate(LAGS):
                if 0 < lag <= len(done) and step < len(done[-lag]):
                    after.append(done[-lag][step])
            if following is not None and k == min(RELAY_AT, usual - 1):
                received, relayed = gather_rows(own, row_count, [])
                after += relayed[:1]
            if s > 0 and k == usual - 1:
                place(s - 1)
            arrived, terms = slot_sum(s, k, (high, low), after)
            done.append(arrived)
            parts[s].append(terms)
            if k == 0:
                others.append(rest(s, (high, low)))
    place(members - 1)
    rows_all = placed[-1][0]

    panel = None
    panel_parts = []
    for s in range(members):
        if exchange:
            swapped = swap_col(split_halves(core, pieces[s]), 1, col_count)
            panel = place_panel(col_place, pieces[s], swapped, s, members, panel)
        else:
            outgoing = rows_all[s].reshape(out_rows, col_count, rows_out)
            arrived = lax.all_to_all(outgoing, "col", split_axis=1, concat_axis=0, tiled=True)
            panel_parts.append(arrived.reshape(width, rows_out).T)
    if not exchange:
        panel = jnp.stack(panel_parts)
    return panel, rows_all


def solution(mesh):
    in_specs = (P("row", "col"), P(None, "row", "col"), P())
    out_specs = (P(None, ("row", "col"), None), P(None, "col", "row"))
    return jax.shard_map(
        per_device, mesh=mesh, in_specs=in_specs, out_specs=out_specs, check_vma=False
    )
```

```python
import functools

import jax
import jax.numpy as jnp
from jax import lax
from jax.experimental import pallas as pl
from jax.experimental.pallas import tpu as pltpu
from jax.sharding import PartitionSpec as P

BS = 1280
F32 = jnp.float32
BF16 = jnp.bfloat16
I32 = jnp.int32
VMEM_LIMIT = 20 * 1024 * 1024
PARAMS = pltpu.CompilerParams(vmem_limit_bytes=VMEM_LIMIT)
LAGS = (2, 3, 5)
PRODUCT_FLOPS = 0
RELAY_AT = 2
ANY = pl.BlockSpec(memory_space=pl.ANY)


def tile_of(extent, wanted, step):
    best = extent
    for size in range(step, wanted + 1, step):
        if extent % size == 0:
            best = size
    return best


def cost(bytes_accessed):
    return pl.CostEstimate(flops=0, bytes_accessed=bytes_accessed, transcendentals=0)


def copy_kernel(source, target):
    target[...] = source[0]


def share_of(factor_rows, member):
    share, cols = factor_rows.shape[1:]
    return pl.pallas_call(
        copy_kernel,
        grid=(1,),
        in_specs=[pl.BlockSpec((1, share, cols), lambda i: (member, 0, 0))],
        out_specs=pl.BlockSpec((share, cols), lambda i: (0, 0)),
        out_shape=jax.ShapeDtypeStruct((share, cols), F32),
        compiler_params=PARAMS,
        cost_estimate=cost(1024),
        name="own_share",
    )(factor_rows)


def prep_kernel(places, share, following, base, units, bits, meta_ref, *refs):
    pieces = refs[: len(places)]
    rest = refs[len(places) :]
    if following:
        next_in, high_ref, low_ref, next_out, whole = rest
        next_out[...] = next_in[0]
    else:
        high_ref, low_ref, whole = rest
    me = meta_ref[base + 2]
    row = meta_ref[base + 3]
    step = pl.program_id(0)
    rows = whole.shape[0] >> bits
    for (mask, offset), piece in zip(places, pieces):
        first = (row ^ mask) * share + offset
        for at in range(0, piece.shape[0], rows):
            flip = ((first + at) // rows) ^ me
            turned_flip = sum(((flip >> bit) & 1) << (bits - 1 - bit) for bit in range(bits))
            whole[pl.ds(pl.multiple_of(turned_flip * rows, rows), rows), :] = piece[at : at + rows, :]
    scale = jnp.where(meta_ref[base + 4 + step] > 0, -1.0, 0.0).astype(F32)
    turned = whole[...].T * scale
    high = turned.astype(BF16)
    high_ref[...] = high
    low_ref[...] = (turned - high.astype(F32)).astype(BF16)


def prepare(base, meta, factor_rows, own, received, width, unit, bits, following):
    share, cols = own.shape
    units = cols // unit
    places = [(0, 0)] + [(mask, offset) for mask, offset, _ in received]
    arrays = [own] + [piece for _, _, piece in received]
    in_specs = [pl.BlockSpec((piece.shape[0], unit), lambda i, m: (0, i)) for piece in arrays]
    out_specs = [pl.BlockSpec((unit, width), lambda i, m: (i, 0))] * 2
    out_shape = [jax.ShapeDtypeStruct((cols, width), BF16)] * 2
    if following is not None:
        arrays.append(factor_rows)
        in_specs.append(pl.BlockSpec((1, share, unit), lambda i, m: (following, 0, i)))
        out_specs.append(pl.BlockSpec((share, unit), lambda i, m: (0, i)))
        out_shape.append(jax.ShapeDtypeStruct((share, cols), F32))
    outs = pl.pallas_call(
        functools.partial(prep_kernel, places, share, following is not None, base, units, bits),
        grid_spec=pltpu.PrefetchScalarGridSpec(
            num_scalar_prefetch=1,
            grid=(units,),
            in_specs=in_specs,
            out_specs=out_specs,
            scratch_shapes=[pltpu.VMEM((width, unit), F32)],
        ),
        out_shape=out_shape,
        compiler_params=PARAMS,
        cost_estimate=cost(1024),
        name="prepare_factor",
    )(meta, *arrays)
    return outs if following is not None else (*outs, None)


def slot_kernel(base, tile, deps, meta_ref, a_ref, high_ref, low_ref, *refs):
    mine_ref, theirs_ref, buffer, total, arrived = refs[deps:]
    half, rows, block = mine_ref.shape
    tiles = block // tile
    depth = buffer.shape[0]
    first = meta_ref[base] * block

    def copy(t):
        source = a_ref.at[pl.ds(pl.multiple_of(first + t * tile, tile), tile), :]
        slot = lax.rem(t, depth)
        return pltpu.make_async_copy(source, buffer.at[slot], arrived.at[slot])

    def turn(t):
        turned = total[lax.rem(t, 2)].T
        columns = pl.ds(pl.multiple_of(t * tile, tile), tile)
        mine_ref[:, :, columns] = turned[: half * rows].reshape(half, rows, tile)
        theirs_ref[:, :, columns] = turned[half * rows :].reshape(half, rows, tile)

    def product(t):
        a = buffer[lax.rem(t, depth)]
        a_high = a.astype(BF16)
        a_low = (a - a_high.astype(F32)).astype(BF16)
        dot = functools.partial(jnp.dot, preferred_element_type=F32)
        total[lax.rem(t, 2)] = (
            dot(a_high, high_ref[...]) + dot(a_high, low_ref[...]) + dot(a_low, high_ref[...])
        )

    valid = meta_ref[base + 1] > 0

    @pl.when(valid)
    def _():
        for t in range(min(depth - 1, tiles)):
            copy(t).start()

        def step(t, carry):
            @pl.when(t + depth - 1 < tiles)
            def _():
                copy(t + depth - 1).start()

            copy(t).wait()
            product(t)
            turn(lax.max(t - 1, 0))
            return carry

        lax.fori_loop(0, tiles, step, 0)
        turn(tiles - 1)

    @pl.when(jnp.logical_not(valid))
    def _():
        mine_ref[...] = jnp.zeros_like(mine_ref)
        theirs_ref[...] = jnp.zeros_like(theirs_ref)


def slot_product(base, meta, ancestor, high, low, chunks, block, after):
    cols, width = high.shape
    tile = tile_of(block, 256, 128)
    rows = width // chunks
    half = chunks // 2
    in_vmem = pl.BlockSpec(memory_space=pltpu.VMEM)
    return pl.pallas_call(
        functools.partial(slot_kernel, base, tile, len(after)),
        grid_spec=pltpu.PrefetchScalarGridSpec(
            num_scalar_prefetch=1,
            grid=(1,),
            in_specs=[ANY, in_vmem, in_vmem] + [ANY] * len(after),
            out_specs=[in_vmem, in_vmem],
            scratch_shapes=[
                pltpu.VMEM((3, tile, cols), F32),
                pltpu.VMEM((2, tile, width), F32),
                pltpu.SemaphoreType.DMA((3,)),
            ],
        ),
        out_shape=[jax.ShapeDtypeStruct((half, rows, block), F32)] * 2,
        compiler_params=PARAMS,
        cost_estimate=pl.CostEstimate(
            flops=PRODUCT_FLOPS, bytes_accessed=4 * block * cols, transcendentals=0
        ),
        name="slot_product",
    )(meta, ancestor, high, low, *after)


def place_kernel(base, fields, terms, ignored, meta_ref, *refs):
    count = len(terms)
    parts = [refs[sum(terms[:k]) : sum(terms[: k + 1])] for k in range(count)]
    outs = refs[sum(terms) + ignored :]
    rows_ref, sends = outs[0], outs[1:]
    groups = rows_ref.shape[2] // parts[0][0].shape[2]
    block = parts[0][0].shape[2]
    place = meta_ref[base + 2] // 2
    rows_ref[...] = jnp.zeros_like(rows_ref)
    for send in sends:
        send[...] = jnp.zeros_like(send)
    for k in range(count):
        at = meta_ref[base + k * fields]

        @pl.when(meta_ref[base + k * fields + 1] > 0)
        def _(k=k, at=at):
            total = parts[k][0][0]
            for term in parts[k][1:]:
                total = total + term[0]
            for g in range(groups):

                @pl.when(at == g)
                def _():
                    rows_ref[0, :, g * block : (g + 1) * block] = total

            for flip, send in enumerate(sends):

                @pl.when(at == (place ^ flip))
                def _():
                    send[...] = total


def place_slots(base, fields, meta, parts, member, members, previous, local_rows, line, exchange, after):
    rows, block = parts[0][0].shape[1:]
    terms = [len(part) for part in parts]
    arrays = [term for part in parts for term in part]
    first = pl.BlockSpec((1, rows, block), lambda i, meta_ref: (0, 0, 0))
    in_specs = [first] * len(arrays)
    aliases = {}
    if previous is not None:
        aliases = {1 + len(arrays): 0}
        arrays.append(previous)
        in_specs.append(ANY)
    arrays += after
    in_specs += [ANY] * len(after)
    ignored = len(after) + (previous is not None)
    out_specs = [pl.BlockSpec((1, rows, local_rows), lambda i, meta_ref: (member, 0, 0))]
    out_shape = [jax.ShapeDtypeStruct((members, rows, local_rows), F32)]
    if exchange:
        out_specs += [pl.BlockSpec((rows, block), lambda i, meta_ref: (0, 0))] * line
        out_shape += [jax.ShapeDtypeStruct((rows, block), F32)] * line
    return pl.pallas_call(
        functools.partial(place_kernel, base, fields, terms, ignored),
        grid_spec=pltpu.PrefetchScalarGridSpec(
            num_scalar_prefetch=1, grid=(1,), in_specs=in_specs, out_specs=out_specs
        ),
        out_shape=out_shape,
        input_output_aliases=aliases,
        compiler_params=PARAMS,
        cost_estimate=cost(1024),
        name="place_slots",
    )(meta, *arrays)


def split_kernel(core_ref, *refs):
    pieces, out = refs[:-1], refs[-1]
    half = out.shape[2]
    for at, piece in enumerate(pieces):
        for core in range(2):

            @pl.when(core_ref[0] == core)
            def _():
                out[at] = piece[:, (1 - core) * half : (2 - core) * half]


def split_halves(core, pieces):
    rows, block = pieces[0].shape
    whole = pl.BlockSpec((rows, block), lambda i, core_ref: (0, 0))
    shape = (len(pieces), rows, block // 2)
    return pl.pallas_call(
        split_kernel,
        grid_spec=pltpu.PrefetchScalarGridSpec(
            num_scalar_prefetch=1,
            grid=(1,),
            in_specs=[whole] * len(pieces),
            out_specs=pl.BlockSpec(shape, lambda i, core_ref: (0, 0, 0)),
        ),
        out_shape=jax.ShapeDtypeStruct(shape, F32),
        compiler_params=PARAMS,
        cost_estimate=cost(1024),
        name="split_halves",
    )(core.reshape(1), *pieces)


def panel_kernel(line, col_ref, *refs):
    pieces, swapped, out, whole = refs[:line], refs[line], refs[-2], refs[-1]
    rows = pieces[0].shape[0]
    half = swapped.shape[2]
    me = col_ref[0]
    core = me % 2
    for flip, piece in enumerate(pieces):
        for side in range(2):

            @pl.when(core == side)
            def _():
                first = pl.multiple_of((me ^ (2 * flip)) * rows, rows)
                whole[pl.ds(first, rows), :] = piece[:, side * half : (side + 1) * half]

        first = pl.multiple_of((me ^ (2 * flip + 1)) * rows, rows)
        whole[pl.ds(first, rows), :] = swapped[flip]
    out[0] = whole[...].T


def place_panel(col_place, pieces, swapped, member, members, previous):
    line = len(pieces)
    rows, block = pieces[0].shape
    half = block // 2
    width = 2 * line * rows
    arrays = list(pieces) + [swapped]
    in_specs = [pl.BlockSpec((rows, block), lambda i, col_ref: (0, 0))] * line
    in_specs.append(pl.BlockSpec(swapped.shape, lambda i, col_ref: (0, 0, 0)))
    aliases = {}
    if previous is not None:
        aliases = {1 + len(arrays): 0}
        arrays.append(previous)
        in_specs.append(ANY)
    return pl.pallas_call(
        functools.partial(panel_kernel, line),
        grid_spec=pltpu.PrefetchScalarGridSpec(
            num_scalar_prefetch=1,
            grid=(1,),
            in_specs=in_specs,
            out_specs=pl.BlockSpec((1, half, width), lambda i, col_ref: (member, 0, 0)),
            scratch_shapes=[pltpu.VMEM((width, half), F32)],
        ),
        out_shape=jax.ShapeDtypeStruct((members, half, width), F32),
        input_output_aliases=aliases,
        compiler_params=PARAMS,
        cost_estimate=cost(1024),
        name="place_panel",
    )(col_place.reshape(1), *arrays)


def halves_kernel(deps, first, second, *refs):
    first_out, second_out = refs[deps:]
    first_out[...] = first[...]
    second_out[...] = second[...]


def gather_rows(mine, count, after):
    half, cols = mine.shape[0] // 2, mine.shape[1]
    pieces = {}
    received, relayed = [], []

    def swap(value, mask):
        return lax.ppermute(value, "row", [(i, i ^ mask) for i in range(count)])

    for mask in sorted(range(1, count), key=lambda m: m.bit_count()):
        if mask.bit_count() == 1:
            whole = swap(mine, mask)
            pieces[mask] = ((whole, 0), (whole, 1))
            received.append((mask, 0, whole))
        else:
            least = mask & -mask
            most = 1 << (mask.bit_length() - 1)
            first, first_at = pieces[mask ^ most][0]
            second, second_at = pieces[mask ^ least][1]
            out = pl.BlockSpec((half, cols), lambda i: (0, 0))
            first, second = pl.pallas_call(
                functools.partial(halves_kernel, len(after)),
                grid=(1,),
                in_specs=[
                    pl.BlockSpec((half, cols), lambda i, at=first_at: (at, 0)),
                    pl.BlockSpec((half, cols), lambda i, at=second_at: (at, 0)),
                ]
                + [ANY] * len(after),
                out_specs=[out, out],
                out_shape=[jax.ShapeDtypeStruct((half, cols), F32)] * 2,
                compiler_params=PARAMS,
                cost_estimate=cost(1024),
                name="relay_halves",
            )(first, second, *after)
            relayed += [first, second]
            first, second = swap(first, most), swap(second, least)
            pieces[mask] = ((first, 0), (second, 0))
            received.append((mask, 0, first))
            received.append((mask, half, second))
    return received, relayed


def swap_col(value, flip, count):
    return lax.ppermute(value, "col", [(c, c ^ flip) for c in range(count)])


def halved_sum(mine, theirs, count):
    arrived = [swap_col(theirs, 1, count)]
    terms = [mine, arrived[0]]
    flip = 2
    while flip < count:
        half = terms[-1].shape[0] // 2
        payload = sum(term[half : 2 * half] for term in terms)
        arrived.append(swap_col(payload, flip, count))
        terms.append(arrived[-1])
        flip *= 2
    return arrived, [sum(term[:1] for term in terms[:-1]), terms[-1][:1]]


def listed_in(block_lists, blocks):
    return jnp.any(block_lists[:, :, None] == blocks[None, None, :], axis=1)


def per_device(ancestor, factor_rows, block_lists):
    members, share, local_cols = factor_rows.shape
    local_rows = ancestor.shape[0]
    row_count, col_count = lax.axis_size("row"), lax.axis_size("col")
    row_place, col_place = lax.axis_index("row"), lax.axis_index("col")
    width = share * row_count
    line = col_count // 2
    core = col_place % 2
    block = min(BS, local_rows)
    groups = local_rows // block
    unit = min(BS, local_cols)
    units = local_cols // unit
    rows_out = local_rows // col_count
    exchange = 2 * rows_out == block
    bits = col_count.bit_length() - 1

    row_blocks = (row_place * local_rows + block * lax.iota(I32, groups)) // BS
    col_blocks = (col_place * local_cols + unit * lax.iota(I32, units)) // BS
    row_listed = listed_in(block_lists, row_blocks)
    col_listed = listed_in(block_lists, col_blocks).astype(I32)
    rank = jnp.cumsum(row_listed.astype(I32), axis=1) - 1
    slots = lax.iota(I32, groups)
    chosen = row_listed[:, None, :] & (rank[:, None, :] == slots[None, :, None])
    slot_block = jnp.sum(chosen * slots[None, None, :], axis=2)
    slot_valid = jnp.any(chosen, axis=2)
    fields = 4 + units
    meta = jnp.concatenate(
        [
            slot_block[:, :, None],
            slot_valid[:, :, None].astype(I32),
            jnp.broadcast_to(col_place, (members, groups, 1)).astype(I32),
            jnp.broadcast_to(row_place, (members, groups, 1)).astype(I32),
            jnp.broadcast_to(col_listed[:, None, :], (members, groups, units)),
        ],
        axis=2,
    ).reshape(-1)

    usual = groups if groups <= 1 else groups - 1
    group_of = block_lists * BS // local_rows
    held = jnp.sum(group_of[:, :, None] == lax.iota(I32, row_count)[None, None, :], axis=1)
    fullest = jnp.max(held, axis=1)
    out_rows = width // col_count

    def slot_sum(s, k, factors, after):
        base = (s * groups + k) * fields
        mine, theirs = slot_product(base, meta, ancestor, *factors, col_count, block, after)
        return halved_sum(mine, theirs, col_count)

    def rest(s, factors):
        def taken():
            return [sum(slot_sum(s, k, factors, [])[1]) for k in range(usual, groups)]

        def left():
            return [jnp.zeros((1, out_rows, block), F32) for _ in range(usual, groups)]

        if usual == groups:
            return []
        return [[total] for total in lax.cond(fullest[s] > usual, taken, left)]

    def exchange_of(placed):
        pieces = [placed[1]]
        for flip in range(line - 1, 0, -1):
            pieces.insert(1, swap_col(placed[1 + flip], 2 * flip, col_count))
        return pieces

    done, parts, others, placed, pieces = [], [], [], [], []

    def place(s):
        placed.append(
            place_slots(
                s * groups * fields,
                fields,
                meta,
                parts[s] + others[s],
                s,
                members,
                placed[s - 1][0] if s > 0 else None,
                local_rows,
                line,
                exchange,
                [],
            )
        )
        if exchange:
            pieces.append(exchange_of(placed[s]))

    own = share_of(factor_rows, 0)
    received, relayed = gather_rows(own, row_count, [])
    for s in range(members):
        following = s + 1 if s + 1 < members else None
        high, low, own = prepare(
            s * groups * fields, meta, factor_rows, own, received, width, unit, bits, following
        )
        parts.append([])
        for k in range(usual):
            after = []
            for step, lag in enumerate(LAGS):
                if 0 < lag <= len(done) and step < len(done[-lag]):
                    after.append(done[-lag][step])
            if following is not None and k == min(RELAY_AT, usual - 1):
                received, relayed = gather_rows(own, row_count, [])
                after += relayed[:1]
            if s > 0 and k == usual - 1:
                place(s - 1)
            arrived, terms = slot_sum(s, k, (high, low), after)
            done.append(arrived)
            parts[s].append(terms)
            if k == 0:
                others.append(rest(s, (high, low)))
    place(members - 1)
    rows_all = placed[-1][0]

    panel = None
    panel_parts = []
    for s in range(members):
        if exchange:
            swapped = swap_col(split_halves(core, pieces[s]), 1, col_count)
            panel = place_panel(col_place, pieces[s], swapped, s, members, panel)
        else:
            outgoing = rows_all[s].reshape(out_rows, col_count, rows_out)
            arrived = lax.all_to_all(outgoing, "col", split_axis=1, concat_axis=0, tiled=True)
            panel_parts.append(arrived.reshape(width, rows_out).T)
    if not exchange:
        panel = jnp.stack(panel_parts)
    return panel, rows_all


def solution(mesh):
    in_specs = (P("row", "col"), P(None, "row", "col"), P())
    out_specs = (P(None, ("row", "col"), None), P(None, "col", "row"))
    return jax.shard_map(
        per_device, mesh=mesh, in_specs=in_specs, out_specs=out_specs, check_vma=False
    )
```
